32 devices in a mesh: ka: 16 (over z, y, x), br: 2 (over core).
Axes of the slice: x: 2, y: 2, z: 4, core: 2. Of those that a mesh axis runs over, the one named last changes fastest.
Arguments:
- occupation: float32 [8, 8192], P(None, 'ka'), may hold values from 0 to 1
- phonons: float32 [12, 4096], P('br', 'ka'), may hold values from 0.05 to 5
- coupling: bfloat16 [16, 12, 8, 8, 8192], P(None, 'br', None, None, 'ka'), may hold values from 0.00049972534 to 0.0079956055
- shifted_point_index: int32 [16, 8192], P(None, 'ka'), may hold values from 0 to 8191
- wavevector_index: int32 [16, 8192], P(None, 'ka'), may hold values from 0 to 4095
- window: int32 [8, 8192], P(None, 'ka'), may hold values 0 or 1
Outputs:
- collision: float32 [8, 8192], P(None, 'ka')
- generation: float32 [12, 4096], P('br', 'ka')
The draws below stay inside these ranges and needn't reach their ends.
All inputs are finite; a program needn't handle non-finite values. No bound on the sum of `window` on one device may be relied on, other than what follows from the above.
Results may differ from the reference program's by a relative error of at most 0.0003.
Values sent between devices are 32-bit elements; how exact they have to be, the bound alone decides.
A program may use at most 128 MiB of HBM per device.

```python
import math
import jax
import jax.numpy as jnp
from jax import lax

NB = 8
NBR = 12
QSUB = 4096
QPK = 16
NK = 8192


def with_ends(values, stream_key, smallest, high):
    dims = values.shape
    spot = [jax.random.randint(jax.random.fold_in(stream_key, axis), (), 0, dims[axis]) for axis in range(len(dims))]
    values = values.at[tuple(spot)].set(smallest)
    longest = dims.index(max(dims))
    spot[longest] = (spot[longest] + 1) % dims[longest]
    return values.at[tuple(spot)].set(high)


def level_of(stream_key, shape, pieces, low, high):
    def one(position, blocks):
        steps = jax.random.uniform(jax.random.fold_in(jax.random.fold_in(stream_key, 6), position), (blocks,), jnp.float32, low / len(pieces), high / len(pieces))
        return jnp.repeat(jnp.exp(steps), shape[position] // blocks).reshape((-1,) + (1,) * (len(shape) - position - 1))

    loudness = one(*pieces[0])
    for cut in pieces[1:]:
        loudness = loudness * one(*cut)
    return loudness


def setup_inputs(seed: int = 0) -> dict:
    keys = jax.random.split(jax.random.key(seed), 7)
    return {
        "occupation": jnp.clip(1.0 * jax.random.uniform(keys[0], (NB, NK), jnp.float32) ** level_of(keys[0], (NB, NK), ((1, 16),), -0.2, 0.2), 0.0, 1.0),
        "phonons": jnp.clip(jnp.exp(math.log(5.0) - 4.6051702 * jax.random.uniform(keys[1], (NBR, QSUB), jnp.float32) ** level_of(keys[1], (NBR, QSUB), ((0, 2), (1, 16)), -0.2, 0.2)), 0.05, 5.0),
        "coupling": jnp.clip(jnp.exp(math.log(0.0079956055) - 2.7725887 * jax.random.uniform(keys[2], (QPK, NBR, NB, NB, NK), jnp.float32) ** level_of(keys[2], (QPK, NBR, NB, NB, NK), ((1, 2), (4, 16)), -0.2, 0.2)), 0.00049972534, 0.0079956055).astype(jnp.bfloat16),
        "shifted_point_index": with_ends(jax.random.randint(keys[3], (QPK, NK), 0, NK), jax.random.fold_in(keys[3], 1), 0, NK - 1).astype(jnp.int32),
        "wavevector_index": with_ends(jax.random.randint(keys[4], (QPK, NK), 0, QSUB), jax.random.fold_in(keys[4], 1), 0, QSUB - 1).astype(jnp.int32),
        "window": with_ends((jax.random.randint(keys[5], (NB, NK), 0, 4) < 3).astype(jnp.int32), jax.random.fold_in(keys[5], 1), 0, 1),
    }


def apply_scattering(occupation, phonons, coupling, shifted_point_index, wavevector_index, window):
    window_f = window.astype(jnp.float32)

    def slot_step(loop_state, inputs):
        scattering_sum, emission_sum = loop_state
        tile, k_plus, q_rows = inputs
        tile = tile.astype(jnp.float32)
        beyond = occupation[:, k_plus]
        phonon_at = phonons[:, q_rows]
        weighted = jnp.einsum("umnk,nk->umk", tile, beyond)
        totals = jnp.sum(tile, axis=2)
        detailed_balance_term = window_f[None] * (weighted * (phonon_at[:, None, :] + 1.0) - occupation[None] * weighted - occupation[None] * totals * phonon_at[:, None, :])
        per_point = jnp.sum(detailed_balance_term, axis=1)
        collected_values = jax.ops.segment_sum(per_point.T, q_rows, num_segments=QSUB).T
        return (scattering_sum + jnp.sum(detailed_balance_term, axis=0), emission_sum + collected_values), None

    start = (jnp.zeros(occupation.shape, jnp.float32), jnp.zeros(phonons.shape, jnp.float32))
    result, _ = lax.scan(slot_step, start, (coupling, shifted_point_index, wavevector_index))
    return result[0], result[1] / 16.0


def reference(occupation, phonons, coupling, shifted_point_index, wavevector_index, window):
    initial_scattering, initial_emission = apply_scattering(occupation, phonons, coupling, shifted_point_index, wavevector_index, window)
    halfway_occupancy = occupation + 0.1 * initial_scattering
    mid_phonons = phonons + 0.1 * initial_emission
    collision, generation = apply_scattering(halfway_occupancy, mid_phonons, coupling, shifted_point_index, wavevector_index, window)
    return collision, generation
```

```python
import functools

import jax
import jax.numpy as jnp
from jax import lax
from jax.experimental import pallas as pl
from jax.experimental.pallas import tpu as pltpu
from jax.sharding import PartitionSpec as P

MESH = pl.DeviceIdType.MESH
F32 = jnp.float32
BF16 = jnp.bfloat16
LANES = 128


def quotient(x, size):
    if size & (size - 1) == 0:
        return lax.shift_right_logical(x, jnp.int32(size.bit_length() - 1))
    return lax.div(x, jnp.int32(size))


def remainder(x, size):
    if size & (size - 1) == 0:
        return lax.bitwise_and(x, jnp.int32(size - 1))
    return lax.rem(x, jnp.int32(size))


def split_terms(x):
    high = x.astype(BF16).astype(F32)
    return high, x - high


def step_kernel(
    n, nbr, branches,
    occ_ref, pho_ref, coup_hbm, kidx_ref, qidx_ref, win_ref,
    col_ref, gen_ref,
    coup, onehot_k, onehot_q, f_all, p_all, g_send, g_recv, c_send, c_recv,
    f_terms, p_terms, c_acc, g_acc, wf, ww,
    load_sem, fs_sem, fr_sem, ws_sem, wr_sem, ps_sem, pr_sem, gs_sem, gr_sem, cs_sem, cr_sem,
):
    me = lax.axis_index("ka")
    core = lax.axis_index("br")
    slots, bands, width = coup.shape[0], occ_ref.shape[0], occ_ref.shape[1]
    piece = width // nbr
    q_width = pho_ref.shape[1]
    rows = 8

    def load(s):
        return pltpu.make_async_copy(coup_hbm.at[s], coup.at[s], load_sem.at[s])

    def start_load(s, c):
        load(s).start()
        return c

    lax.fori_loop(0, slots, start_load, 0)

    def ahead(j):
        return lax.rem(me + j, n)

    def behind(j):
        return lax.rem(me - j + n, n)

    sibling = {"br": 1 - core}

    barrier = pltpu.get_barrier_semaphore()

    def greet(j, c):
        pl.semaphore_signal(barrier, inc=1, device_id={"ka": ahead(j)}, device_id_type=MESH)
        return c

    lax.fori_loop(1, n, greet, 0)
    pl.semaphore_signal(barrier, inc=1, device_id=sibling, device_id_type=MESH)
    pl.semaphore_wait(barrier, n)

    def f_copy(i, j):
        block = f_all.at[i, me, core]
        return pltpu.make_async_remote_copy(
            block, block, fs_sem.at[i, j], fr_sem.at[i, j], device_id={"ka": ahead(j)}, device_id_type=MESH)

    def f_forward(i, j):
        block = f_all.at[i, behind(j), core]
        return pltpu.make_async_remote_copy(
            block, block, ws_sem.at[i, j], wr_sem.at[i, j], device_id=sibling, device_id_type=MESH)

    def p_copy(i, j):
        block = p_all.at[i, me]
        return pltpu.make_async_remote_copy(
            block, block, ps_sem.at[i, j], pr_sem.at[i, j], device_id={"ka": ahead(j)}, device_id_type=MESH)

    def g_copy(i, j):
        return pltpu.make_async_remote_copy(
            g_send.at[i, ahead(j)], g_recv.at[i, me], gs_sem.at[i, j], gr_sem.at[i, j],
            device_id={"ka": ahead(j)}, device_id_type=MESH)

    def c_copy(i):
        return pltpu.make_async_remote_copy(
            c_send.at[i], c_recv.at[i], cs_sem.at[i], cr_sem.at[i], device_id=sibling, device_id_type=MESH)

    def each(do):
        def body(j, c):
            do(j)
            return c
        lax.fori_loop(1, n, body, 0)

    def send_f(i, f):
        for h in range(nbr):
            f_all[i, me, h] = f[:, h * piece:(h + 1) * piece]
        each(lambda j: f_copy(i, j).start())

    def send_p(i, p):
        p_all[i, me] = p
        each(lambda j: p_copy(i, j).start())

    def pass_on_f(i):
        def forward(j):
            f_copy(i, j).wait_recv()
            f_forward(i, j).start()
        each(forward)

    def collect_f(i):
        each(lambda j: f_forward(i, j).wait_recv())

        def body(a, c):
            both = jnp.concatenate([f_all[i, a, h] for h in range(nbr)], axis=0)
            high, low = split_terms(both)
            at = pl.ds(pl.multiple_of(a * nbr * rows, nbr * rows), nbr * rows)
            f_terms[0, at] = high.astype(BF16)
            f_terms[1, at] = low.astype(BF16)
            return c
        lax.fori_loop(0, n, body, 0)

    def collect_p(i):
        each(lambda j: p_copy(i, j).wait_recv())

        def body(a, c):
            both = jnp.concatenate([p_all[i, 2 * a], p_all[i, 2 * a + 1]], axis=0)
            high, low = split_terms(both)
            at = pl.ds(pl.multiple_of(a * 2 * rows, 2 * rows), 2 * rows)
            p_terms[0, at] = high.astype(BF16)
            p_terms[1, at] = low.astype(BF16)
            return c
        lax.fori_loop(0, n // 2, body, 0)

    def scatter_pass(i, f, window):
        for m in range(bands):
            ww[m] = jnp.broadcast_to(window[m:m + 1], (rows, width))
            wf[m] = jnp.broadcast_to((window * f)[m:m + 1], (rows, width))
        c_acc[...] = jnp.zeros_like(c_acc)
        g_acc[...] = jnp.zeros_like(g_acc)

        def body(s, carry):
            if i == 0:
                load(s).wait()
            k_high = quotient(kidx_ref[pl.ds(s, 1), :], piece)
            q_index = qidx_ref[pl.ds(s, 1), :]
            q_high = quotient(q_index, q_width)
            chunk = 2 * LANES
            for k0 in range(0, width, chunk):
                at = slice(k0, k0 + chunk)
                lk = onehot_k[s, :, at]
                lq = onehot_q[s, :, at]
                picked = jnp.dot(f_terms[0], lk, preferred_element_type=F32) + jnp.dot(
                    f_terms[1], lk, preferred_element_type=F32)
                kh = jnp.broadcast_to(k_high[:, at], (rows, chunk))
                e = jnp.zeros((rows, chunk), F32)
                for h in range(n * nbr):
                    e = jnp.where(kh == h, picked[h * rows:(h + 1) * rows], e)
                picked = jnp.dot(p_terms[0], lq, preferred_element_type=F32) + jnp.dot(
                    p_terms[1], lq, preferred_element_type=F32)
                qh = jnp.broadcast_to(q_high[:, at], (rows, chunk))
                w = jnp.zeros((rows, chunk), F32)
                for h in range(n):
                    w = jnp.where(qh == h, picked[h * rows:(h + 1) * rows], w)

                sums = []
                for k1 in range(0, chunk, LANES):
                    here = slice(k0 + k1, k0 + k1 + LANES)
                    e1 = e[:, k1:k1 + LANES]
                    w1 = w[:, k1:k1 + LANES]
                    row = lax.broadcasted_iota(jnp.int32, (rows, LANES), 0)
                    acc = [c_acc[m, :, here] for m in range(bands)]
                    t = jnp.zeros((rows, LANES), F32)
                    for u in range(branches):
                        wu = jnp.broadcast_to(w1[u:u + 1], (rows, LANES))
                        x = e1 * (wu + 1.0)
                        y = e1 + wu
                        total = None
                        for m in range(0, bands, 2):
                            first = (u * bands + m) * rows
                            g2 = coup[s, first:first + 2 * rows, here].astype(F32)
                            for d in range(2):
                                term = g2[d * rows:(d + 1) * rows] * (
                                    ww[m + d, :, here] * x - wf[m + d, :, here] * y)
                                acc[m + d] = acc[m + d] + term
                                total = term if total is None else total + term
                        t = jnp.where(row == u, jnp.sum(total, axis=0, keepdims=True), t)
                    for m in range(bands):
                        c_acc[m, :, here] = acc[m]
                    sums.append(t)
                t = jnp.concatenate(sums, axis=1)
                parts = [
                    jnp.where(qh == h, part, 0.0) for part in split_terms(t) for h in range(n)]
                spread = jnp.concatenate(parts, axis=0).astype(BF16)
                g_acc[...] += lax.dot_general(
                    spread, lq, (((1,), (1,)), ((), ())), preferred_element_type=F32)
            return carry

        lax.fori_loop(0, slots, body, 0)

        total = (g_acc[:n * rows] + g_acc[n * rows:]) * (1.0 / 16.0)
        g_send[i] = total.reshape(n, rows, q_width)
        each(lambda j: g_copy(i, j).start())
        mine = jnp.concatenate(
            [jnp.sum(c_acc[m], axis=0, keepdims=True) for m in range(bands)], axis=0)
        c_send[i] = mine
        c_copy(i).start()
        c_copy(i).wait_recv()
        return mine + c_recv[i]

    def finish_g(i):
        each(lambda j: g_copy(i, j).wait_recv())
        g_recv[i, me] = g_send[i, me]
        return jnp.sum(g_recv[i], axis=0)

    f0 = occ_ref[...]
    window = win_ref[...].astype(F32)
    send_f(0, f0)
    p0 = jnp.concatenate([pho_ref[...], jnp.zeros((rows - branches, q_width), F32)], axis=0)
    send_p(0, p0)

    def build(s, c):
        low_k = remainder(kidx_ref[pl.ds(s, 1), :], piece)
        low_q = remainder(qidx_ref[pl.ds(s, 1), :], q_width)
        onehot_k[s] = jnp.where(
            lax.broadcasted_iota(jnp.int32, (piece, width), 0) == low_k, 1.0, 0.0).astype(BF16)
        onehot_q[s] = jnp.where(
            lax.broadcasted_iota(jnp.int32, (q_width, width), 0) == low_q, 1.0, 0.0).astype(BF16)
        return c

    pass_on_f(0)
    lax.fori_loop(0, slots, build, 0)
    collect_f(0)
    collect_p(0)
    c0 = scatter_pass(0, f0, window)
    f1 = f0 + 0.1 * c0
    send_f(1, f1)
    p1 = p0 + 0.1 * finish_g(0)
    send_p(1, p1)
    pass_on_f(1)
    collect_f(1)
    collect_p(1)
    col_ref[...] = scatter_pass(1, f1, window)
    gen_ref[...] = finish_g(1)[:branches]

    def drain(j, c):
        for i in range(2):
            f_copy(i, j).wait_send()
            f_forward(i, j).wait_send()
            p_copy(i, j).wait_send()
            g_copy(i, j).wait_send()
        return c

    lax.fori_loop(1, n, drain, 0)
    for i in range(2):
        c_copy(i).wait_send()


def solution(mesh):
    n, nbr = mesh.shape["ka"], mesh.shape["br"]

    def on_device(occupation, phonons, coupling, shifted_point_index, wavevector_index, window):
        slots, branches, bands, _, width = coupling.shape
        q_width = phonons.shape[1]
        piece = width // nbr
        rows = 8
        coupling = coupling.reshape(slots, branches * bands * bands, width)
        vmem = pl.BlockSpec(memory_space=pltpu.VMEM)
        return pl.pallas_call(
            functools.partial(step_kernel, n, nbr, branches),
            out_shape=(
                jax.ShapeDtypeStruct((bands, width), F32),
                jax.ShapeDtypeStruct((branches, q_width), F32),
            ),
            in_specs=[vmem, vmem, pl.BlockSpec(memory_space=pl.ANY), vmem, vmem, vmem],
            out_specs=(vmem, vmem),
            scratch_shapes=[
                pltpu.VMEM(coupling.shape, BF16),
                pltpu.VMEM((slots, piece, width), BF16),
                pltpu.VMEM((slots, q_width, width), BF16),
                pltpu.VMEM((2, n, nbr, rows, piece), F32),
                pltpu.VMEM((2, n, rows, q_width), F32),
                pltpu.VMEM((2, n, rows, q_width), F32),
                pltpu.VMEM((2, n, rows, q_width), F32),
                pltpu.VMEM((2, bands, width), F32),
                pltpu.VMEM((2, bands, width), F32),
                pltpu.VMEM((2, n * nbr * rows, piece), BF16),
                pltpu.VMEM((2, n * rows, q_width), BF16),
                pltpu.VMEM((bands, rows, width), F32),
                pltpu.VMEM((2 * n * rows, q_width), F32),
                pltpu.VMEM((bands, rows, width), F32),
                pltpu.VMEM((bands, rows, width), F32),
                pltpu.SemaphoreType.DMA((slots,)),
            ] + [pltpu.SemaphoreType.DMA((2, n))] * 8 + [pltpu.SemaphoreType.DMA((2,))] * 2,
            compiler_params=pltpu.CompilerParams(
                collective_id=0, has_side_effects=True, vmem_limit_bytes=48 * 1024 * 1024),
            cost_estimate=pl.CostEstimate(
                flops=40 * coupling.size, bytes_accessed=2 * coupling.size, transcendentals=0),
        )(occupation, phonons, coupling, shifted_point_index, wavevector_index, window)

    return jax.shard_map(
        on_device,
        mesh=mesh,
        in_specs=(
            P(None, "ka"), P("br", "ka"), P(None, "br", None, None, "ka"),
            P(None, "ka"), P(None, "ka"), P(None, "ka"),
        ),
        out_specs=(P(None, "ka"), P("br", "ka")),
        check_vma=False,
    )
```

```python
import functools

import jax
import jax.numpy as jnp
from jax import lax
from jax.experimental import pallas as pl
from jax.experimental.pallas import tpu as pltpu
from jax.sharding import PartitionSpec as P

MESH = pl.DeviceIdType.MESH
F32 = jnp.float32
BF16 = jnp.bfloat16
LANES = 128


def quotient(x, size):
    if size & (size - 1) == 0:
        return lax.shift_right_logical(x, jnp.int32(size.bit_length() - 1))
    return lax.div(x, jnp.int32(size))


def remainder(x, size):
    if size & (size - 1) == 0:
        return lax.bitwise_and(x, jnp.int32(size - 1))
    return lax.rem(x, jnp.int32(size))


def split_terms(x):
    high = x.astype(BF16).astype(F32)
    return high, x - high


def step_kernel(
    n, nbr, branches,
    occ_hbm, pho_hbm, coup_hbm, kidx_hbm, qidx_hbm, win_hbm,
    col_ref, gen_ref,
    occ, pho, kidx, qidx, win,
    coup, onehot_k, onehot_q, f_all, p_all, g_send, g_recv, c_send, c_recv,
    f_terms, p_terms, c_acc, g_acc, wf, ww,
    in_sem, load_sem, fs_sem, fr_sem, ws_sem, wr_sem, ps_sem, pr_sem, gs_sem, gr_sem, cs_sem, cr_sem,
):
    me = lax.axis_index("ka")
    core = lax.axis_index("br")
    slots, bands, width = coup.shape[0], occ.shape[0], occ.shape[1]
    piece = width // nbr
    q_width = pho.shape[1]
    rows = 8

    inputs = [
        pltpu.make_async_copy(src, dst, in_sem.at[a])
        for a, (src, dst) in enumerate(
            ((occ_hbm, occ), (pho_hbm, pho), (qidx_hbm, qidx), (kidx_hbm, kidx), (win_hbm, win)))]
    for copy in inputs:
        copy.start()

    def load(s):
        return pltpu.make_async_copy(coup_hbm.at[s], coup.at[s], load_sem.at[s])

    def start_load(s, c):
        load(s).start()
        return c

    def ahead(j):
        return lax.rem(me + j, n)

    def behind(j):
        return lax.rem(me - j + n, n)

    sibling = {"br": 1 - core}

    barrier = pltpu.get_barrier_semaphore()

    def greet(j, c):
        pl.semaphore_signal(barrier, inc=1, device_id={"ka": ahead(j)}, device_id_type=MESH)
        return c

    lax.fori_loop(1, n, greet, 0)
    pl.semaphore_signal(barrier, inc=1, device_id=sibling, device_id_type=MESH)
    lax.fori_loop(0, slots, start_load, 0)
    for copy in inputs:
        copy.wait()
    pl.semaphore_wait(barrier, n)

    def f_copy(i, j):
        block = f_all.at[i, me, core]
        return pltpu.make_async_remote_copy(
            block, block, fs_sem.at[i, j], fr_sem.at[i, j], device_id={"ka": ahead(j)}, device_id_type=MESH)

    def f_forward(i, j):
        block = f_all.at[i, behind(j), core]
        return pltpu.make_async_remote_copy(
            block, block, ws_sem.at[i, j], wr_sem.at[i, j], device_id=sibling, device_id_type=MESH)

    def p_copy(i, j):
        block = p_all.at[i, me]
        return pltpu.make_async_remote_copy(
            block, block, ps_sem.at[i, j], pr_sem.at[i, j], device_id={"ka": ahead(j)}, device_id_type=MESH)

    def g_copy(i, j):
        return pltpu.make_async_remote_copy(
            g_send.at[i, ahead(j)], g_recv.at[i, me], gs_sem.at[i, j], gr_sem.at[i, j],
            device_id={"ka": ahead(j)}, device_id_type=MESH)

    def c_copy(i):
        return pltpu.make_async_remote_copy(
            c_send.at[i], c_recv.at[i], cs_sem.at[i], cr_sem.at[i], device_id=sibling, device_id_type=MESH)

    def each(do):
        def body(j, c):
            do(j)
            return c
        lax.fori_loop(1, n, body, 0)

    def send_f(i, f):
        for h in range(nbr):
            f_all[i, me, h] = f[:, h * piece:(h + 1) * piece]
        each(lambda j: f_copy(i, j).start())

    def send_p(i, p):
        p_all[i, me] = p
        each(lambda j: p_copy(i, j).start())

    def pass_on_f(i):
        def forward(j):
            f_copy(i, j).wait_recv()
            f_forward(i, j).start()
        each(forward)

    def collect_f(i):
        each(lambda j: f_forward(i, j).wait_recv())

        def body(a, c):
            both = jnp.concatenate([f_all[i, a, h] for h in range(nbr)], axis=0)
            high, low = split_terms(both)
            at = pl.ds(pl.multiple_of(a * nbr * rows, nbr * rows), nbr * rows)
            f_terms[at] = high.astype(BF16)
            at = pl.ds(pl.multiple_of((n + a) * nbr * rows, nbr * rows), nbr * rows)
            f_terms[at] = low.astype(BF16)
            return c
        lax.fori_loop(0, n, body, 0)

    def collect_p(i):
        each(lambda j: p_copy(i, j).wait_recv())

        def body(a, c):
            both = jnp.concatenate([p_all[i, 2 * a], p_all[i, 2 * a + 1]], axis=0)
            high, low = split_terms(both)
            at = pl.ds(pl.multiple_of(a * 2 * rows, 2 * rows), 2 * rows)
            p_terms[at] = high.astype(BF16)
            at = pl.ds(pl.multiple_of((n + 2 * a) * rows, 2 * rows), 2 * rows)
            p_terms[at] = low.astype(BF16)
            return c
        lax.fori_loop(0, n // 2, body, 0)

    def scatter_pass(i, f, window):
        for m in range(bands):
            ww[m] = jnp.broadcast_to(window[m:m + 1], (rows, width))
            wf[m] = jnp.broadcast_to((window * f)[m:m + 1], (rows, width))
        c_acc[...] = jnp.zeros_like(c_acc)
        g_acc[...] = jnp.zeros_like(g_acc)

        def select(picked, at, count):
            half = count * rows
            index = jnp.broadcast_to(at, (rows, width))
            out = picked[:rows] + picked[half:half + rows]
            for h in range(1, count):
                first = h * rows
                here = picked[first:first + rows] + picked[half + first:half + first + rows]
                out = jnp.where(index == h, here, out)
            return out

        def gather(s):
            picked = jnp.dot(f_terms[...], onehot_k[s], preferred_element_type=F32)
            e = select(picked, quotient(kidx[pl.ds(s, 1), :], piece), n * nbr)
            picked = jnp.dot(p_terms[...], onehot_q[s], preferred_element_type=F32)
            w = select(picked, quotient(qidx[pl.ds(s, 1), :], q_width), n)
            return e, w

        def terms(s, e, w):
            sums = []
            row = lax.broadcasted_iota(jnp.int32, (rows, LANES), 0)
            for k0 in range(0, width, LANES):
                here = slice(k0, k0 + LANES)
                e1 = e[:, here]
                w1 = w[:, here]
                acc = [c_acc[m, :, here] for m in range(bands)]
                t = jnp.zeros((rows, LANES), F32)
                for u in range(branches):
                    wu = jnp.broadcast_to(w1[u:u + 1], (rows, LANES))
                    x = e1 * (wu + 1.0)
                    y = e1 + wu
                    total = None
                    for m in range(0, bands, 2):
                        first = (u * bands + m) * rows
                        g2 = coup[s, first:first + 2 * rows, here].astype(F32)
                        for d in range(2):
                            term = g2[d * rows:(d + 1) * rows] * (
                                ww[m + d, :, here] * x - wf[m + d, :, here] * y)
                            acc[m + d] = acc[m + d] + term
                            total = term if total is None else total + term
                    t = jnp.where(row == u, jnp.sum(total, axis=0, keepdims=True), t)
                for m in range(bands):
                    c_acc[m, :, here] = acc[m]
                sums.append(t)
            return jnp.concatenate(sums, axis=1)

        def scatter(s, t):
            index = jnp.broadcast_to(quotient(qidx[pl.ds(s, 1), :], q_width), (rows, width))
            parts = [jnp.where(index == h, part, 0.0) for part in split_terms(t) for h in range(n)]
            spread = jnp.concatenate(parts, axis=0).astype(BF16)
            g_acc[...] += lax.dot_general(
                spread, onehot_q[s], (((1,), (1,)), ((), ())), preferred_element_type=F32)

        def body(s, carry):
            e, w, t = carry
            if i == 0:
                load(s).wait()
            after = gather(jnp.minimum(s + 1, slots - 1))
            fresh = terms(s, e, w)
            scatter(jnp.maximum(s - 1, 0), t)
            return after + (fresh,)

        first = gather(0) + (jnp.zeros((rows, width), F32),)
        _, _, t = lax.fori_loop(0, slots, body, first)
        scatter(slots - 1, t)

        total = (g_acc[:n * rows] + g_acc[n * rows:]) * (1.0 / 16.0)
        g_send[i] = total.reshape(n, rows, q_width)
        each(lambda j: g_copy(i, j).start())
        mine = jnp.concatenate(
            [jnp.sum(c_acc[m], axis=0, keepdims=True) for m in range(bands)], axis=0)
        c_send[i] = mine
        c_copy(i).start()
        c_copy(i).wait_recv()
        return mine + c_recv[i]

    def finish_g(i):
        each(lambda j: g_copy(i, j).wait_recv())
        g_recv[i, me] = g_send[i, me]
        return jnp.sum(g_recv[i], axis=0)

    f0 = occ[...]
    window = win[...].astype(F32)
    send_f(0, f0)
    p0 = jnp.concatenate([pho[...], jnp.zeros((rows - branches, q_width), F32)], axis=0)
    send_p(0, p0)

    def build_q(s, c):
        low = remainder(qidx[pl.ds(s, 1), :], q_width)
        onehot_q[s] = jnp.where(
            lax.broadcasted_iota(jnp.int32, (q_width, width), 0) == low, 1.0, 0.0).astype(BF16)
        return c

    def build_k(s, c):
        low = remainder(kidx[pl.ds(s, 1), :], piece)
        onehot_k[s] = jnp.where(
            lax.broadcasted_iota(jnp.int32, (piece, width), 0) == low, 1.0, 0.0).astype(BF16)
        return c

    lax.fori_loop(0, slots, build_q, 0)
    pass_on_f(0)
    lax.fori_loop(0, slots, build_k, 0)
    collect_f(0)
    collect_p(0)
    c0 = scatter_pass(0, f0, window)
    f1 = f0 + 0.1 * c0
    send_f(1, f1)
    p1 = p0 + 0.1 * finish_g(0)
    send_p(1, p1)
    pass_on_f(1)
    collect_f(1)
    collect_p(1)
    col_ref[...] = scatter_pass(1, f1, window)
    gen_ref[...] = finish_g(1)[:branches]

    def drain(j, c):
        for i in range(2):
            f_copy(i, j).wait_send()
            f_forward(i, j).wait_send()
            p_copy(i, j).wait_send()
            g_copy(i, j).wait_send()
        return c

    lax.fori_loop(1, n, drain, 0)
    for i in range(2):
        c_copy(i).wait_send()


def solution(mesh):
    n, nbr = mesh.shape["ka"], mesh.shape["br"]

    def on_device(occupation, phonons, coupling, shifted_point_index, wavevector_index, window):
        slots, branches, bands, _, width = coupling.shape
        q_width = phonons.shape[1]
        piece = width // nbr
        rows = 8
        coupling = coupling.reshape(slots, branches * bands * bands, width)
        vmem = pl.BlockSpec(memory_space=pltpu.VMEM)
        return pl.pallas_call(
            functools.partial(step_kernel, n, nbr, branches),
            out_shape=(
                jax.ShapeDtypeStruct((bands, width), F32),
                jax.ShapeDtypeStruct((branches, q_width), F32),
            ),
            in_specs=[pl.BlockSpec(memory_space=pl.ANY)] * 6,
            out_specs=(vmem, vmem),
            scratch_shapes=[
                pltpu.VMEM(occupation.shape, F32),
                pltpu.VMEM(phonons.shape, F32),
                pltpu.VMEM(shifted_point_index.shape, jnp.int32),
                pltpu.VMEM(wavevector_index.shape, jnp.int32),
                pltpu.VMEM(window.shape, jnp.int32),
                pltpu.VMEM(coupling.shape, BF16),
                pltpu.VMEM((slots, piece, width), BF16),
                pltpu.VMEM((slots, q_width, width), BF16),
                pltpu.VMEM((2, n, nbr, rows, piece), F32),
                pltpu.VMEM((2, n, rows, q_width), F32),
                pltpu.VMEM((2, n, rows, q_width), F32),
                pltpu.VMEM((2, n, rows, q_width), F32),
                pltpu.VMEM((2, bands, width), F32),
                pltpu.VMEM((2, bands, width), F32),
                pltpu.VMEM((2 * n * nbr * rows, piece), BF16),
                pltpu.VMEM((2 * n * rows, q_width), BF16),
                pltpu.VMEM((bands, rows, width), F32),
                pltpu.VMEM((2 * n * rows, q_width), F32),
                pltpu.VMEM((bands, rows, width), F32),
                pltpu.VMEM((bands, rows, width), F32),
                pltpu.SemaphoreType.DMA((5,)),
                pltpu.SemaphoreType.DMA((slots,)),
            ] + [pltpu.SemaphoreType.DMA((2, n))] * 8 + [pltpu.SemaphoreType.DMA((2,))] * 2,
            compiler_params=pltpu.CompilerParams(
                collective_id=0, has_side_effects=True, vmem_limit_bytes=63 * 1024 * 1024),
            cost_estimate=pl.CostEstimate(
                flops=40 * coupling.size, bytes_accessed=2 * coupling.size, transcendentals=0),
        )(occupation, phonons, coupling, shifted_point_index, wavevector_index, window)

    return jax.shard_map(
        on_device,
        mesh=mesh,
        in_specs=(
            P(None, "ka"), P("br", "ka"), P(None, "br", None, None, "ka"),
            P(None, "ka"), P(None, "ka"), P(None, "ka"),
        ),
        out_specs=(P(None, "ka"), P("br", "ka")),
        check_vma=False,
    )
```

```python
import functools

import jax
import jax.numpy as jnp
from jax import lax
from jax.experimental import pallas as pl
from jax.experimental.pallas import tpu as pltpu
from jax.sharding import PartitionSpec as P

MESH = pl.DeviceIdType.MESH
F32 = jnp.float32
BF16 = jnp.bfloat16
LANES = 128


def quotient(x, size):
    if size & (size - 1) == 0:
        return lax.shift_right_logical(x, jnp.int32(size.bit_length() - 1))
    return lax.div(x, jnp.int32(size))


def remainder(x, size):
    if size & (size - 1) == 0:
        return lax.bitwise_and(x, jnp.int32(size - 1))
    return lax.rem(x, jnp.int32(size))


def split_terms(x):
    high = x.astype(BF16).astype(F32)
    return high, x - high


def step_kernel(
    n, nbr, branches,
    occ_hbm, pho_hbm, coup_hbm, kidx_hbm, qidx_hbm, win_hbm,
    col_ref, gen_ref,
    occ, pho, kidx, qidx, win,
    coup, onehot_q, f_all, p_all, g_send, g_recv, c_send, c_recv,
    p_terms, c_acc, g_acc, wf, ww,
    in_sem, load_sem, fs_sem, fr_sem, ws_sem, wr_sem, ps_sem, pr_sem, gs_sem, gr_sem, cs_sem, cr_sem,
):
    me = lax.axis_index("ka")
    core = lax.axis_index("br")
    slots, bands, width = coup.shape[0], occ.shape[0], occ.shape[1]
    piece = width // nbr
    q_width = pho.shape[1]
    rows = 8

    inputs = [
        pltpu.make_async_copy(src, dst, in_sem.at[a])
        for a, (src, dst) in enumerate(
            ((occ_hbm, occ), (pho_hbm, pho), (qidx_hbm, qidx), (kidx_hbm, kidx), (win_hbm, win)))]
    for copy in inputs:
        copy.start()

    def load(s):
        return pltpu.make_async_copy(coup_hbm.at[s], coup.at[s], load_sem.at[s])

    def start_load(s, c):
        load(s).start()
        return c

    def ahead(j):
        return lax.rem(me + j, n)

    def behind(j):
        return lax.rem(me - j + n, n)

    sibling = {"br": 1 - core}

    barrier = pltpu.get_barrier_semaphore()

    def greet(j, c):
        pl.semaphore_signal(barrier, inc=1, device_id={"ka": ahead(j)}, device_id_type=MESH)
        return c

    lax.fori_loop(1, n, greet, 0)
    pl.semaphore_signal(barrier, inc=1, device_id=sibling, device_id_type=MESH)
    lax.fori_loop(0, slots, start_load, 0)
    for copy in inputs:
        copy.wait()
    pl.semaphore_wait(barrier, n)

    def f_copy(i, j):
        block = f_all.at[i, me, core]
        return pltpu.make_async_remote_copy(
            block, block, fs_sem.at[i, j], fr_sem.at[i, j], device_id={"ka": ahead(j)}, device_id_type=MESH)

    def f_forward(i, j):
        block = f_all.at[i, behind(j), core]
        return pltpu.make_async_remote_copy(
            block, block, ws_sem.at[i, j], wr_sem.at[i, j], device_id=sibling, device_id_type=MESH)

    def p_copy(i, j):
        block = p_all.at[i, me]
        return pltpu.make_async_remote_copy(
            block, block, ps_sem.at[i, j], pr_sem.at[i, j], device_id={"ka": ahead(j)}, device_id_type=MESH)

    def g_copy(i, j):
        return pltpu.make_async_remote_copy(
            g_send.at[i, ahead(j)], g_recv.at[i, me], gs_sem.at[i, j], gr_sem.at[i, j],
            device_id={"ka": ahead(j)}, device_id_type=MESH)

    def c_copy(i):
        return pltpu.make_async_remote_copy(
            c_send.at[i], c_recv.at[i], cs_sem.at[i], cr_sem.at[i], device_id=sibling, device_id_type=MESH)

    def each(do):
        def body(j, c):
            do(j)
            return c
        lax.fori_loop(1, n, body, 0)

    def send_f(i, f):
        for h in range(nbr):
            f_all[i, me, h] = f[:, h * piece:(h + 1) * piece]
        each(lambda j: f_copy(i, j).start())

    def send_p(i, p):
        p_all[i, me] = p
        each(lambda j: p_copy(i, j).start())

    def pass_on_f(i):
        def forward(j):
            f_copy(i, j).wait_recv()
            f_forward(i, j).start()
        each(forward)

    def collect_f(i):
        each(lambda j: f_forward(i, j).wait_recv())

    def collect_p(i):
        each(lambda j: p_copy(i, j).wait_recv())

        def body(a, c):
            both = jnp.concatenate([p_all[i, 2 * a], p_all[i, 2 * a + 1]], axis=0)
            high, low = split_terms(both)
            at = pl.ds(pl.multiple_of(a * 2 * rows, 2 * rows), 2 * rows)
            p_terms[at] = high.astype(BF16)
            at = pl.ds(pl.multiple_of((n + 2 * a) * rows, 2 * rows), 2 * rows)
            p_terms[at] = low.astype(BF16)
            return c
        lax.fori_loop(0, n // 2, body, 0)

    def scatter_pass(i, f, window):
        for m in range(bands):
            ww[m] = jnp.broadcast_to(window[m:m + 1], (rows, width))
            wf[m] = jnp.broadcast_to((window * f)[m:m + 1], (rows, width))
        c_acc[...] = jnp.zeros_like(c_acc)
        g_acc[...] = jnp.zeros_like(g_acc)

        def select(picked, at, count):
            half = count * rows
            index = jnp.broadcast_to(at, (rows, width))
            out = picked[:rows] + picked[half:half + rows]
            for h in range(1, count):
                first = h * rows
                here = picked[first:first + rows] + picked[half + first:half + first + rows]
                out = jnp.where(index == h, here, out)
            return out

        def gather(s):
            k_index = kidx[pl.ds(s, 1), :]
            columns = []
            for k0 in range(0, width, LANES):
                at = jnp.broadcast_to(k_index[:, k0:k0 + LANES], (rows, LANES))
                lane, group = remainder(at, LANES), quotient(at, LANES)
                e = jnp.zeros((rows, LANES), F32)
                for h in range(n * width // LANES):
                    owner, rest = divmod(h * LANES, width)
                    half, first = divmod(rest, piece)
                    block = f_all[i, owner, half, :, first:first + LANES]
                    found = jnp.take_along_axis(block, lane, axis=1, mode="promise_in_bounds")
                    e = jnp.where(group == h, found, e)
                columns.append(e)
            e = jnp.concatenate(columns, axis=1)
            picked = jnp.dot(p_terms[...], onehot_q[s], preferred_element_type=F32)
            w = select(picked, quotient(qidx[pl.ds(s, 1), :], q_width), n)
            return e, w

        def terms(s, e, w):
            sums = []
            row = lax.broadcasted_iota(jnp.int32, (rows, LANES), 0)
            for k0 in range(0, width, LANES):
                here = slice(k0, k0 + LANES)
                e1 = e[:, here]
                w1 = w[:, here]
                acc = [c_acc[m, :, here] for m in range(bands)]
                t = jnp.zeros((rows, LANES), F32)
                for u in range(branches):
                    wu = jnp.broadcast_to(w1[u:u + 1], (rows, LANES))
                    x = e1 * (wu + 1.0)
                    y = e1 + wu
                    total = None
                    for m in range(0, bands, 2):
                        first = (u * bands + m) * rows
                        g2 = coup[s, first:first + 2 * rows, here].astype(F32)
                        for d in range(2):
                            term = g2[d * rows:(d + 1) * rows] * (
                                ww[m + d, :, here] * x - wf[m + d, :, here] * y)
                            acc[m + d] = acc[m + d] + term
                            total = term if total is None else total + term
                    t = jnp.where(row == u, jnp.sum(total, axis=0, keepdims=True), t)
                for m in range(bands):
                    c_acc[m, :, here] = acc[m]
                sums.append(t)
            return jnp.concatenate(sums, axis=1)

        def scatter(s, t):
            index = jnp.broadcast_to(quotient(qidx[pl.ds(s, 1), :], q_width), (rows, width))
            parts = [jnp.where(index == h, part, 0.0) for part in split_terms(t) for h in range(n)]
            spread = jnp.concatenate(parts, axis=0).astype(BF16)
            g_acc[...] += lax.dot_general(
                spread, onehot_q[s], (((1,), (1,)), ((), ())), preferred_element_type=F32)

        def body(s, carry):
            e, w, t = carry
            if i == 0:
                load(s).wait()
            after = gather(jnp.minimum(s + 1, slots - 1))
            fresh = terms(s, e, w)
            scatter(jnp.maximum(s - 1, 0), t)
            return after + (fresh,)

        first = gather(0) + (jnp.zeros((rows, width), F32),)
        _, _, t = lax.fori_loop(0, slots, body, first)
        scatter(slots - 1, t)

        total = (g_acc[:n * rows] + g_acc[n * rows:]) * (1.0 / 16.0)
        g_send[i] = total.reshape(n, rows, q_width)
        each(lambda j: g_copy(i, j).start())
        mine = jnp.concatenate(
            [jnp.sum(c_acc[m], axis=0, keepdims=True) for m in range(bands)], axis=0)
        c_send[i] = mine
        c_copy(i).start()
        c_copy(i).wait_recv()
        return mine + c_recv[i]

    def finish_g(i):
        each(lambda j: g_copy(i, j).wait_recv())
        g_recv[i, me] = g_send[i, me]
        return jnp.sum(g_recv[i], axis=0)

    f0 = occ[...]
    window = win[...].astype(F32)
    send_f(0, f0)
    p0 = jnp.concatenate([pho[...], jnp.zeros((rows - branches, q_width), F32)], axis=0)
    send_p(0, p0)

    def build_q(s, c):
        low = remainder(qidx[pl.ds(s, 1), :], q_width)
        onehot_q[s] = jnp.where(
            lax.broadcasted_iota(jnp.int32, (q_width, width), 0) == low, 1.0, 0.0).astype(BF16)
        return c

    lax.fori_loop(0, slots, build_q, 0)
    pass_on_f(0)
    collect_f(0)
    collect_p(0)
    c0 = scatter_pass(0, f0, window)
    f1 = f0 + 0.1 * c0
    send_f(1, f1)
    p1 = p0 + 0.1 * finish_g(0)
    send_p(1, p1)
    pass_on_f(1)
    collect_f(1)
    collect_p(1)
    col_ref[...] = scatter_pass(1, f1, window)
    gen_ref[...] = finish_g(1)[:branches]

    def drain(j, c):
        for i in range(2):
            f_copy(i, j).wait_send()
            f_forward(i, j).wait_send()
            p_copy(i, j).wait_send()
            g_copy(i, j).wait_send()
        return c

    lax.fori_loop(1, n, drain, 0)
    for i in range(2):
        c_copy(i).wait_send()


def solution(mesh):
    n, nbr = mesh.shape["ka"], mesh.shape["br"]

    def on_device(occupation, phonons, coupling, shifted_point_index, wavevector_index, window):
        slots, branches, bands, _, width = coupling.shape
        q_width = phonons.shape[1]
        piece = width // nbr
        rows = 8
        coupling = coupling.reshape(slots, branches * bands * bands, width)
        vmem = pl.BlockSpec(memory_space=pltpu.VMEM)
        return pl.pallas_call(
            functools.partial(step_kernel, n, nbr, branches),
            out_shape=(
                jax.ShapeDtypeStruct((bands, width), F32),
                jax.ShapeDtypeStruct((branches, q_width), F32),
            ),
            in_specs=[pl.BlockSpec(memory_space=pl.ANY)] * 6,
            out_specs=(vmem, vmem),
            scratch_shapes=[
                pltpu.VMEM(occupation.shape, F32),
                pltpu.VMEM(phonons.shape, F32),
                pltpu.VMEM(shifted_point_index.shape, jnp.int32),
                pltpu.VMEM(wavevector_index.shape, jnp.int32),
                pltpu.VMEM(window.shape, jnp.int32),
                pltpu.VMEM(coupling.shape, BF16),
                pltpu.VMEM((slots, q_width, width), BF16),
                pltpu.VMEM((2, n, nbr, rows, piece), F32),
                pltpu.VMEM((2, n, rows, q_width), F32),
                pltpu.VMEM((2, n, rows, q_width), F32),
                pltpu.VMEM((2, n, rows, q_width), F32),
                pltpu.VMEM((2, bands, width), F32),
                pltpu.VMEM((2, bands, width), F32),
                pltpu.VMEM((2 * n * rows, q_width), BF16),
                pltpu.VMEM((bands, rows, width), F32),
                pltpu.VMEM((2 * n * rows, q_width), F32),
                pltpu.VMEM((bands, rows, width), F32),
                pltpu.VMEM((bands, rows, width), F32),
                pltpu.SemaphoreType.DMA((5,)),
                pltpu.SemaphoreType.DMA((slots,)),
            ] + [pltpu.SemaphoreType.DMA((2, n))] * 8 + [pltpu.SemaphoreType.DMA((2,))] * 2,
            compiler_params=pltpu.CompilerParams(
                collective_id=0, has_side_effects=True, vmem_limit_bytes=63 * 1024 * 1024),
            cost_estimate=pl.CostEstimate(
                flops=40 * coupling.size, bytes_accessed=2 * coupling.size, transcendentals=0),
        )(occupation, phonons, coupling, shifted_point_index, wavevector_index, window)

    return jax.shard_map(
        on_device,
        mesh=mesh,
        in_specs=(
            P(None, "ka"), P("br", "ka"), P(None, "br", None, None, "ka"),
            P(None, "ka"), P(None, "ka"), P(None, "ka"),
        ),
        out_specs=(P(None, "ka"), P("br", "ka")),
        check_vma=False,
    )
```
